32 devices in a mesh: seq: 8 (over z, y), ch: 4 (over x, core).
Axes of the slice: x: 2, y: 2, z: 4, core: 2. Of those that a mesh axis runs over, the one named last changes fastest.
Arguments:
- query_stream: bfloat16 [2048, 4096], P('seq', 'ch'), may hold values from -6 to 6
- key_stream: bfloat16 [2048, 4096], P('seq', 'ch'), may hold values from -6 to 6
- value_stream: bfloat16 [2048, 4096], P('seq', 'ch'), may hold values from -6 to 6
- filter_taps: float32 [4096, 128], P('ch'), may hold values from -0.5 to 0.5
- out_weight: bfloat16 [4096, 4096], P('seq', 'ch'), may hold values from -0.09375 to 0.09375
- upstream: bfloat16 [2048, 4096], P('seq', 'ch'), may hold values from -6 to 6
Outputs:
- mixed: bfloat16 [2048, 4096], P('seq', 'ch')
- grad_query: bfloat16 [2048, 4096], P('seq', 'ch')
- grad_key: bfloat16 [2048, 4096], P('seq', 'ch')
- grad_value: bfloat16 [2048, 4096], P('seq', 'ch')
- grad_filter: float32 [4096, 128], P('ch')
- grad_weight: float32 [4096, 4096], P('seq', 'ch')
The draws below stay inside these ranges and needn't reach their ends.
All inputs are finite; a program needn't handle non-finite values.
Results may differ from the reference program's by a relative error of at most 0.0057.
Values may be sent and summed in bfloat16 or wider, within the bound.
A program may use at most 128 MiB of HBM per device.

```python
import jax
import jax.numpy as jnp
from jax import lax

WIDTH = 4096
CHANNELS = 4096
TAPS = 128
LENGTH = 2048


def with_spikes(result, own_key, source, target, parts, factor):
    def block_of(position):
        return (jnp.arange(result.shape[position]) // (result.shape[position] // parts)).reshape((-1,) + (1,) * (result.ndim - 1 - position))

    one_side = jax.random.permutation(own_key, parts)[block_of(target)]
    other_side = (block_of(target) + parts // 2) % parts
    return jnp.where((block_of(source) == one_side) | (block_of(source) == other_side), factor * result, result)


def level_of(own_key, extent, split, low, high):
    gain = 1.0
    for dim, parts in split:
        draws = jax.random.uniform(jax.random.fold_in(jax.random.fold_in(own_key, 6), dim), (parts,), jnp.float32, low / len(split), high / len(split))
        gain = gain * jnp.repeat(jnp.exp(draws), extent[dim] // parts).reshape((-1,) + (1,) * (len(extent) - 1 - dim))
    return gain


def bell_draw(stream_key, extent, spread, reach, split=(), kind=jnp.bfloat16):
    drawn = jax.random.normal(stream_key, extent, jnp.float32) * spread
    if len(split) > 0:
        drawn = level_of(stream_key, extent, split, -0.22, 0.18) * drawn
    return jnp.clip(drawn, min=-reach, max=reach).astype(kind)


def gaussian_with(stream_key, extent, spread, limit, cuts, heavy, kind=jnp.bfloat16):
    values = spread * jax.random.normal(stream_key, extent, jnp.float32)
    if cuts:
        values = values * level_of(stream_key, extent, cuts, -0.22, 0.18)
    return jnp.clip(with_spikes(values, jax.random.fold_in(stream_key, 3), *heavy), -limit, limit).astype(kind)


def setup_inputs(seed: int = 0) -> dict:
    keys = jax.random.split(jax.random.key(seed), 7)
    return {
        "query_stream": gaussian_with(keys[0], (LENGTH, CHANNELS), 1.0, 6.0, ((0, 8), (1, 4)), (0, 1, 8, 2.0)),
        "key_stream": bell_draw(keys[1], (LENGTH, CHANNELS), 1.0, 6.0, ((0, 8), (1, 4))),
        "value_stream": bell_draw(keys[2], (LENGTH, CHANNELS), 1.0, 6.0, ((0, 8), (1, 4))),
        "filter_taps": bell_draw(keys[3], (CHANNELS, TAPS), TAPS ** -0.5, 0.5, ((0, 4),), jnp.float32),
        "out_weight": bell_draw(keys[4], (CHANNELS, WIDTH), CHANNELS ** -0.5, 0.09375, ((0, 8), (1, 4))),
        "upstream": bell_draw(keys[5], (LENGTH, WIDTH), 1.0, 6.0, ((0, 8), (1, 4))),
    }


def reference(query_stream, key_stream, value_stream, filter_taps, out_weight, upstream):
    length = query_stream.shape[0]
    keyed = (key_stream.astype(jnp.float32) * value_stream.astype(jnp.float32)).astype(jnp.bfloat16)
    front_pad = jnp.concatenate([jnp.zeros((TAPS - 1, CHANNELS), jnp.float32), keyed.astype(jnp.float32)], axis=0)

    def forward_tap(index, accum):
        shifted = lax.dynamic_slice_in_dim(front_pad, TAPS - 1 - index, length, 0)
        column = lax.dynamic_slice_in_dim(filter_taps, index, 1, 1)[:, 0]
        return accum + column[None, :] * shifted

    response = lax.fori_loop(jnp.int32(0), jnp.int32(TAPS), forward_tap, jnp.zeros((length, CHANNELS), jnp.float32))
    gated = (query_stream.astype(jnp.float32) * response).astype(jnp.bfloat16)
    mixed = jnp.dot(gated, out_weight, preferred_element_type=jnp.float32).astype(jnp.bfloat16)
    grad_gated = jnp.dot(upstream, out_weight.T, preferred_element_type=jnp.float32)
    grad_query = (grad_gated * response).astype(jnp.bfloat16)
    grad_response = grad_gated * query_stream.astype(jnp.float32)
    back_pad = jnp.concatenate([grad_response, jnp.zeros((TAPS - 1, CHANNELS), jnp.float32)], axis=0)

    def backward_tap(index, accum):
        shifted = lax.dynamic_slice_in_dim(back_pad, index, length, 0)
        column = lax.dynamic_slice_in_dim(filter_taps, index, 1, 1)[:, 0]
        return accum + column[None, :] * shifted

    grad_keyed = lax.fori_loop(jnp.int32(0), jnp.int32(TAPS), backward_tap, jnp.zeros((length, CHANNELS), jnp.float32))
    grad_key = (grad_keyed * value_stream.astype(jnp.float32)).astype(jnp.bfloat16)
    grad_value = (grad_keyed * key_stream.astype(jnp.float32)).astype(jnp.bfloat16)

    def tap_gradient(index):
        shifted = lax.dynamic_slice_in_dim(front_pad, TAPS - 1 - index, length, 0)
        return jnp.sum(grad_response * shifted, axis=0)

    grad_filter = lax.map(tap_gradient, jnp.arange(TAPS, dtype=jnp.int32)).T
    grad_weight = lax.dot_general(gated, upstream, (((0,), (0,)), ((), ())), preferred_element_type=jnp.float32)
    return mixed, grad_query, grad_key, grad_value, grad_filter, grad_weight
```

```python
import jax
import jax.numpy as jnp
from jax import lax
from jax.sharding import PartitionSpec as P


def from_behind(value, axis, steps):
    count = lax.axis_size(axis)
    initial, last = (max(0, -steps), min(count, count - steps))
    return lax.ppermute(value, axis, [(source, source + steps) for source in range(initial, last)])


def depthwise(signal, kernel):
    output = lax.conv_general_dilated(
        signal[None],
        kernel[:, None, :],
        (1,),
        "VALID",
        dimension_numbers=("NWC", "WIO", "NWC"),
        feature_group_count=signal.shape[1],
        precision=lax.Precision.HIGHEST,
    )
    return output[0]


def body(query_stream, key_stream, value_stream, filter_taps, out_weight, upstream):
    rows_here = query_stream.shape[0]
    tap_count = filter_taps.shape[1]
    upstream_full = lax.all_gather(upstream, "seq", axis=0, tiled=True)
    keyed = (key_stream.astype(jnp.float32) * value_stream.astype(jnp.float32)).astype(jnp.bfloat16)
    rim_before = from_behind(keyed[rows_here - (tap_count - 1) :], "seq", 1)
    front_pad = jnp.concatenate([rim_before, keyed], axis=0).astype(jnp.float32)
    response = depthwise(front_pad, filter_taps.T[::-1])
    query_wide = query_stream.astype(jnp.float32)
    gated = (query_wide * response).astype(jnp.bfloat16)

    partial_terms = lax.dot_general(
        upstream_full, out_weight, (((1,), (1,)), ((), ())), preferred_element_type=jnp.float32
    ).astype(jnp.bfloat16)
    count, width = lax.axis_size("ch"), out_weight.shape[0]
    partial_terms = partial_terms.reshape(-1, count, rows_here // count, width)
    partial_terms = partial_terms.transpose(1, 0, 2, 3).reshape(count, -1, width)
    summed = lax.psum_scatter(partial_terms, "ch", scatter_dimension=0)
    summed = lax.all_to_all(summed, "seq", split_axis=0, concat_axis=1, tiled=True)
    grad_gated = lax.all_to_all(summed, "ch", split_axis=1, concat_axis=0, tiled=True).astype(jnp.float32)

    block = lax.all_to_all(gated, "ch", split_axis=0, concat_axis=1, tiled=True)
    block = lax.all_to_all(block, "seq", split_axis=1, concat_axis=0, tiled=True)
    block = lax.all_gather(block.reshape(-1, rows_here // count, width), "ch", axis=1, tiled=True)
    block = block.reshape(-1, width)

    mixed_part = jnp.dot(block, out_weight, preferred_element_type=jnp.float32).astype(jnp.bfloat16)
    mixed = lax.psum_scatter(mixed_part, "seq", scatter_dimension=0, tiled=True)
    grad_weight = lax.dot_general(
        block, upstream_full, (((0,), (0,)), ((), ())), preferred_element_type=jnp.float32
    )

    grad_query = (grad_gated * response).astype(jnp.bfloat16)
    grad_response = grad_gated * query_wide
    rim_after = from_behind(grad_response[: tap_count - 1], "seq", -1)
    filter_local = depthwise(front_pad, grad_response)[::-1].T
    grad_filter = lax.psum(filter_local, "seq")
    back_pad = jnp.concatenate([grad_response, rim_after], axis=0)
    grad_keyed = depthwise(back_pad, filter_taps.T)
    grad_key = (grad_keyed * value_stream.astype(jnp.float32)).astype(jnp.bfloat16)
    grad_value = (grad_keyed * key_stream.astype(jnp.float32)).astype(jnp.bfloat16)
    return (mixed, grad_query, grad_key, grad_value, grad_filter, grad_weight)


def solution(mesh):
    in_specs = (
        P("seq", "ch"),
        P("seq", "ch"),
        P("seq", "ch"),
        P("ch", None),
        P("seq", "ch"),
        P("seq", "ch"),
    )
    out_specs = (
        P("seq", "ch"),
        P("seq", "ch"),
        P("seq", "ch"),
        P("seq", "ch"),
        P("ch", None),
        P("seq", "ch"),
    )
    return jax.shard_map(body, mesh=mesh, in_specs=in_specs, out_specs=out_specs, check_vma=False)
```

```python
import functools

import jax
import jax.numpy as jnp
from jax import lax
from jax.experimental import pallas as pl
from jax.experimental.pallas import tpu as pltpu
from jax.sharding import PartitionSpec as P

MESH = pl.DeviceIdType.MESH


def remote(src, dst, send, recv, device):
    return pltpu.make_async_remote_copy(
        src_ref=src, dst_ref=dst, send_sem=send, recv_sem=recv, device_id=device, device_id_type=MESH
    )


def greet(devices):
    barrier = pltpu.get_barrier_semaphore()
    for device in devices:
        pl.semaphore_signal(barrier, inc=1, device_id=device, device_id_type=MESH)


def gather_kernel(n, m, per, gated_ref, out_ref, send1, recv1, send2, recv2, local):
    s, h = lax.axis_index("seq"), lax.axis_index("ch")
    quarter = out_ref.shape[2]
    home = s // per
    barrier = pltpu.get_barrier_semaphore()

    def greet_sender(i, _):
        @pl.when(jnp.logical_not(jnp.logical_and(i == s, home == h)))
        def _():
            pl.semaphore_signal(barrier, inc=1, device_id=(i, home), device_id_type=MESH)
        return 0

    lax.fori_loop(0, n, greet_sender, 0)
    for k in range(1, m):
        pl.semaphore_signal(barrier, inc=1, device_id=(s, lax.rem(h + k, m)), device_id_type=MESH)
    pl.semaphore_wait(barrier, per * m + m - 1 - jnp.where(home == h, 1, 0))

    def part(p, k):
        g = lax.rem(h + k, m)
        src = gated_ref.at[p, pl.ds(pl.multiple_of(g * quarter, quarter), quarter)]
        return src, h * per + p, g

    def send(i, _):
        p, k = i // m, i % m
        src, owner, g = part(p, k)
        self = jnp.logical_and(owner == s, k == 0)

        @pl.when(jnp.logical_not(self))
        def _():
            remote(src, out_ref.at[s, g], send1.at[p, k], recv1.at[s], (owner, g)).start()

        @pl.when(self)
        def _():
            pltpu.make_async_copy(src, out_ref.at[s, g], local).start()
        return 0

    lax.fori_loop(0, per * m, send, 0)

    def forward(i, _):
        t = lax.rem(s + i, n)
        block = out_ref.at[t, h]
        self = jnp.logical_and(t == s, home == h)

        @pl.when(jnp.logical_not(self))
        def _():
            remote(block, block, send2.at[0, 0], recv1.at[t], (s, lax.rem(h + 1, m))).wait_recv()

        @pl.when(self)
        def _():
            pltpu.make_async_copy(block, block, local).wait()
        for k in range(1, m):
            remote(block, block, send2.at[t, k - 1], recv2.at[t, k - 1], (s, lax.rem(h + k, m))).start()
        return 0

    lax.fori_loop(0, n, forward, 0)

    def finish(t, _):
        for k in range(1, m):
            block = out_ref.at[t, lax.rem(h + m - k, m)]
            copy = remote(block, block, send2.at[t, k - 1], recv2.at[t, k - 1], (s, lax.rem(h + k, m)))
            copy.wait_recv()
            copy.wait_send()
        return 0

    lax.fori_loop(0, n, finish, 0)

    def drain(i, _):
        p, k = i // m, i % m
        src, owner, g = part(p, k)

        @pl.when(jnp.logical_not(jnp.logical_and(owner == s, k == 0)))
        def _():
            remote(src, out_ref.at[s, g], send1.at[p, k], recv1.at[s], (s, lax.rem(h + 1, m))).wait_send()
        return 0

    lax.fori_loop(0, per * m, drain, 0)


def cost(us):
    return pl.CostEstimate(flops=0, bytes_accessed=int(us * 3.6e6), transcendentals=0)


def params(number):
    return pltpu.CompilerParams(
        collective_id=number, has_side_effects=True, vmem_limit_bytes=32 * 2**20
    )


VMEM = pl.BlockSpec(memory_space=pltpu.VMEM)
DMA = pltpu.SemaphoreType.DMA


def exchange_gated(gated, n, m):
    per, rows, width = gated.shape
    return pl.pallas_call(
        functools.partial(gather_kernel, n, m, per),
        out_shape=jax.ShapeDtypeStruct((n, m, rows // m, width), gated.dtype),
        in_specs=[VMEM],
        out_specs=VMEM,
        scratch_shapes=[DMA((per, m)), DMA((n,)), DMA((n, m - 1)), DMA((n, m - 1)), DMA],
        compiler_params=params(1),
        cost_estimate=cost(25),
    )(gated)


def scatter_kernel(n, m, per, part_ref, out_ref, land, stage, send1, recv1, send2, recv2, local):
    s, h = lax.axis_index("seq"), lax.axis_index("ch")
    quarter = part_ref.shape[2]
    home, place = s // per, lax.rem(s, per)
    barrier = pltpu.get_barrier_semaphore()
    inside = home == h

    def greet_sender(i, _):
        owner, g = h * per + i // m, i % m

        @pl.when(jnp.logical_not(jnp.logical_and(owner == s, g == h)))
        def _():
            pl.semaphore_signal(barrier, inc=1, device_id=(owner, g), device_id_type=MESH)
        return 0

    lax.fori_loop(0, per * m, greet_sender, 0)
    for k in range(1, m):
        pl.semaphore_signal(barrier, inc=1, device_id=(s, lax.rem(h + k, m)), device_id_type=MESH)
    pl.semaphore_wait(barrier, n + m - 1 - jnp.where(inside, 1, 0))

    def first(i, k):
        t, g = lax.rem(s + i + 1, n), lax.rem(h + k, m)
        return remote(
            part_ref.at[t, g], land.at[i, k - 1], send1.at[i, k - 1], recv1.at[i, k - 1], (s, g)
        )

    def send(i, _):
        for k in range(1, m):
            first(i, k).start()
        return 0

    lax.fori_loop(0, n, send, 0)
    target = out_ref.at[place, pl.ds(pl.multiple_of(h * quarter, quarter), quarter)]

    def combine(i, _):
        t = lax.rem(s + i + 1, n)
        total = part_ref[t, h].astype(jnp.float32)
        for k in range(1, m):
            first(i, k).wait_recv()
        for k in range(1, m):
            total += land[i, k - 1].astype(jnp.float32)
        stage[i] = total.astype(stage.dtype)
        self = jnp.logical_and(t == s, inside)

        @pl.when(jnp.logical_not(self))
        def _():
            remote(stage.at[i], target, send2.at[i], recv2.at[place, h], (t, home)).start()

        @pl.when(self)
        def _():
            pltpu.make_async_copy(stage.at[i], target, local).start()
        return 0

    lax.fori_loop(0, n, combine, 0)

    def finish(i, _):
        t = lax.rem(s + i + 1, n)
        for k in range(1, m):
            first(i, k).wait_send()
        self = jnp.logical_and(t == s, inside)

        @pl.when(jnp.logical_not(self))
        def _():
            remote(stage.at[i], target, send2.at[i], recv2.at[place, h], (s, lax.rem(h + 1, m))).wait_send()

        @pl.when(self)
        def _():
            pltpu.make_async_copy(stage.at[i], target, local).wait()
        return 0

    lax.fori_loop(0, n, finish, 0)

    def arrive(i, _):
        p, g = i // m, i % m
        landed = out_ref.at[p, pl.ds(pl.multiple_of(g * quarter, quarter), quarter)]

        @pl.when(jnp.logical_not(jnp.logical_and(h * per + p == s, g == h)))
        def _():
            remote(landed, landed, send2.at[0], recv2.at[p, g], (s, lax.rem(h + 1, m))).wait_recv()
        return 0

    lax.fori_loop(0, per * m, arrive, 0)


def exchange_grad(part, per):
    n, m, quarter, width = part.shape
    return pl.pallas_call(
        functools.partial(scatter_kernel, n, m, per),
        out_shape=jax.ShapeDtypeStruct((per, m * quarter, width), part.dtype),
        in_specs=[VMEM],
        out_specs=VMEM,
        scratch_shapes=[
            pltpu.VMEM((n, m - 1, quarter, width), part.dtype),
            pltpu.VMEM((n, quarter, width), part.dtype),
            DMA((n, m - 1)), DMA((n, m - 1)), DMA((n,)), DMA((per, m)), DMA,
        ],
        compiler_params=params(2),
        cost_estimate=cost(25),
    )(part)


def sum_kernel(n, local_ref, out_ref, land, send1, recv1, send2, recv2):
    s, h = lax.axis_index("seq"), lax.axis_index("ch")
    barrier = pltpu.get_barrier_semaphore()

    def peer(i):
        return lax.rem(s + i, n)

    def hello(i, _):
        pl.semaphore_signal(barrier, inc=1, device_id=(peer(i), h), device_id_type=MESH)
        return 0

    lax.fori_loop(1, n, hello, 0)
    pl.semaphore_wait(barrier, n - 1)

    def first(i):
        return remote(
            local_ref.at[peer(i)], land.at[i - 1], send1.at[i - 1], recv1.at[i - 1], (peer(i), h)
        )

    def second(i):
        return remote(out_ref.at[s], out_ref.at[s], send2.at[i - 1], recv2.at[i - 1], (peer(i), h))

    def send(i, _):
        first(i).start()
        return 0

    lax.fori_loop(1, n, send, 0)
    total = local_ref[s]

    def add(i, total):
        first(i).wait_recv()
        return total + land[i - 1]

    out_ref[s] = lax.fori_loop(1, n, add, total)

    def share(i, _):
        second(i).start()
        return 0

    lax.fori_loop(1, n, share, 0)

    def finish(i, _):
        first(i).wait_send()
        second(i).wait_send()
        landed = out_ref.at[lax.rem(s + n - i, n)]
        remote(landed, landed, send2.at[i - 1], recv2.at[i - 1], (peer(i), h)).wait_recv()
        return 0

    lax.fori_loop(1, n, finish, 0)


def sum_over_seq(value, n):
    blocks = value.reshape(n, -1, value.shape[1])
    total = pl.pallas_call(
        functools.partial(sum_kernel, n),
        out_shape=jax.ShapeDtypeStruct(blocks.shape, blocks.dtype),
        in_specs=[VMEM],
        out_specs=VMEM,
        scratch_shapes=[
            pltpu.VMEM((n - 1,) + blocks.shape[1:], blocks.dtype),
            DMA((n - 1,)), DMA((n - 1,)), DMA((n - 1,)), DMA((n - 1,)),
        ],
        compiler_params=params(3),
        cost_estimate=cost(15),
    )(blocks)
    return total.reshape(value.shape)


def from_behind(value, axis, steps):
    count = lax.axis_size(axis)
    initial, last = (max(0, -steps), min(count, count - steps))
    return lax.ppermute(value, axis, [(source, source + steps) for source in range(initial, last)])


def depthwise(signal, kernel):
    output = lax.conv_general_dilated(
        signal[None],
        kernel[:, None, :],
        (1,),
        "VALID",
        dimension_numbers=("NWC", "WIO", "NWC"),
        feature_group_count=signal.shape[1],
        precision=lax.Precision.HIGHEST,
    )
    return output[0]


def body(query_stream, key_stream, value_stream, filter_taps, out_weight, upstream):
    rows, channels = query_stream.shape
    tap_count = filter_taps.shape[1]
    n, m, width = lax.axis_size("seq"), lax.axis_size("ch"), out_weight.shape[0]
    per = channels // width
    upstream_full = lax.all_gather(upstream, "seq", axis=0, tiled=True)
    keyed = (key_stream.astype(jnp.float32) * value_stream.astype(jnp.float32)).astype(jnp.bfloat16)
    rim_before = from_behind(keyed[rows - (tap_count - 1) :], "seq", 1)
    front_pad = jnp.concatenate([rim_before, keyed], axis=0).astype(jnp.float32)
    response = depthwise(front_pad, filter_taps.T[::-1])
    query_wide = query_stream.astype(jnp.float32)
    gated = (query_wide * response).astype(jnp.bfloat16)
    block = exchange_gated(gated.reshape(rows, per, width).transpose(1, 0, 2), n, m)
    block = block.reshape(n * rows, width)
    mixed_part = jnp.dot(block, out_weight, preferred_element_type=jnp.float32).astype(jnp.bfloat16)

    partial_terms = lax.dot_general(
        upstream_full, out_weight, (((1,), (1,)), ((), ())), preferred_element_type=jnp.float32
    ).astype(jnp.bfloat16)
    partial_terms, mixed_part = lax.optimization_barrier((partial_terms, mixed_part))
    mixed = lax.psum_scatter(mixed_part, "seq", scatter_dimension=0, tiled=True)
    grad_gated = exchange_grad(partial_terms.reshape(n, m, rows // m, width), per)
    grad_gated = grad_gated.transpose(1, 0, 2).reshape(rows, channels).astype(jnp.float32)
    grad_query = (grad_gated * response).astype(jnp.bfloat16)
    grad_response = grad_gated * query_wide
    rim_after = from_behind(grad_response[: tap_count - 1], "seq", -1)
    filter_local = depthwise(front_pad, grad_response)[::-1].T
    back_pad = jnp.concatenate([grad_response, rim_after], axis=0)
    grad_keyed = depthwise(back_pad, filter_taps.T)
    filter_local, grad_keyed = lax.optimization_barrier((filter_local, grad_keyed))
    grad_filter = sum_over_seq(filter_local, n)
    grad_key = (grad_keyed * value_stream.astype(jnp.float32)).astype(jnp.bfloat16)
    grad_value = (grad_keyed * key_stream.astype(jnp.float32)).astype(jnp.bfloat16)
    grad_weight = lax.dot_general(
        block, upstream_full, (((0,), (0,)), ((), ())), preferred_element_type=jnp.float32
    )
    return (mixed, grad_query, grad_key, grad_value, grad_filter, grad_weight)


def solution(mesh):
    in_specs = (
        P("seq", "ch"),
        P("seq", "ch"),
        P("seq", "ch"),
        P("ch", None),
        P("seq", "ch"),
        P("seq", "ch"),
    )
    out_specs = (
        P("seq", "ch"),
        P("seq", "ch"),
        P("seq", "ch"),
        P("seq", "ch"),
        P("ch", None),
        P("seq", "ch"),
    )
    return jax.shard_map(body, mesh=mesh, in_specs=in_specs, out_specs=out_specs, check_vma=False)
```

```python
import functools

import jax
import jax.numpy as jnp
from jax import lax
from jax.experimental import pallas as pl
from jax.experimental.pallas import tpu as pltpu
from jax.sharding import PartitionSpec as P

MESH = pl.DeviceIdType.MESH


def remote(src, dst, send, recv, device):
    return pltpu.make_async_remote_copy(
        src_ref=src, dst_ref=dst, send_sem=send, recv_sem=recv, device_id=device, device_id_type=MESH
    )


def greet(devices):
    barrier = pltpu.get_barrier_semaphore()
    for device in devices:
        pl.semaphore_signal(barrier, inc=1, device_id=device, device_id_type=MESH)


PIECES = 2


def gather_kernel(
    n, m, per, gated_ref, up_ref, out_ref, full_ref,
    send1, recv1, send2, recv2, local, send_line, recv_line, send_pair, recv_pair, own,
):
    s, h = lax.axis_index("seq"), lax.axis_index("ch")
    quarter = out_ref.shape[2]
    home = s // per
    barrier = pltpu.get_barrier_semaphore()

    def greet_sender(i, _):
        @pl.when(jnp.logical_not(jnp.logical_and(i == s, home == h)))
        def _():
            pl.semaphore_signal(barrier, inc=1, device_id=(i, home), device_id_type=MESH)
        return 0

    lax.fori_loop(0, n, greet_sender, 0)
    for k in range(1, m):
        pl.semaphore_signal(barrier, inc=1, device_id=(s, lax.rem(h + k, m)), device_id_type=MESH)
    other = s + 1 - 2 * lax.rem(s, 2)
    has_before, has_after = s >= 2, s < n - 2

    pl.semaphore_signal(barrier, inc=1, device_id=(other, h), device_id_type=MESH)

    @pl.when(has_before)
    def _():
        pl.semaphore_signal(barrier, inc=1, device_id=(s - 2, h), device_id_type=MESH)

    @pl.when(has_after)
    def _():
        pl.semaphore_signal(barrier, inc=1, device_id=(s + 2, h), device_id_type=MESH)

    lines = jnp.where(has_before, 1, 0) + jnp.where(has_after, 1, 0)
    pl.semaphore_wait(barrier, per * m + m - jnp.where(home == h, 1, 0) + lines)

    height = up_ref.shape[0] // PIECES

    def shard(t, c):
        return full_ref.at[t, pl.ds(c * height, height)]

    def along(src, t, way, d, c):
        return remote(
            src, shard(t, c), send_line.at[way, d, c], recv_line.at[way, d + 1, c], (s + 2 - 4 * way, h)
        )

    def across(src, t, c):
        return remote(src, shard(t, c), send_pair.at[t // 2, c], recv_pair.at[t // 2, c], (other, h))

    def begin():
        for c in range(PIECES):
            src = up_ref.at[pl.ds(c * height, height)]
            for way, more in enumerate((has_after, has_before)):

                @pl.when(more)
                def _():
                    along(src, s, way, 0, c).start()

            across(src, s, c).start()
        pltpu.make_async_copy(up_ref, full_ref.at[s], own).start()

    def hop(d, _):
        for c in range(PIECES):
            for way, more in enumerate((has_after, has_before)):
                t = s - (2 - 4 * way) * d

                @pl.when(jnp.logical_and(t >= 0, t < n))
                def _():
                    block = shard(t, c)
                    remote(
                        block, block, send_line.at[way, 0, c], recv_line.at[way, d, c], (other, h)
                    ).wait_recv()

                    @pl.when(more)
                    def _():
                        along(block, t, way, d, c).start()

                    across(block, t, c).start()
        return 0

    def settle(d, _):
        for c in range(PIECES):
            for way, more in enumerate((has_after, has_before)):
                t = s - (2 - 4 * way) * d

                @pl.when(jnp.logical_and(jnp.logical_and(t >= 0, t < n), more))
                def _():
                    along(shard(t, c), t, way, d, c).wait_send()

            sent = lax.rem(s, 2) + 2 * d
            across(shard(sent, c), sent, c).wait_send()
            landed = lax.rem(other, 2) + 2 * d
            across(shard(landed, c), landed, c).wait_recv()
        return 0

    def part(p, k):
        g = lax.rem(h + k, m)
        src = gated_ref.at[p, pl.ds(pl.multiple_of(g * quarter, quarter), quarter)]
        return src, h * per + p, g

    def send(i, _):
        p, k = i // m, i % m
        src, owner, g = part(p, k)
        self = jnp.logical_and(owner == s, k == 0)

        @pl.when(jnp.logical_not(self))
        def _():
            remote(src, out_ref.at[s, g], send1.at[p, k], recv1.at[s], (owner, g)).start()

        @pl.when(self)
        def _():
            pltpu.make_async_copy(src, out_ref.at[s, g], local).start()
        return 0

    lax.fori_loop(0, per * m, send, 0)
    begin()
    lax.fori_loop(1, 2, hop, 0)

    def forward(i, _):
        t = lax.rem(s + i, n)
        block = out_ref.at[t, h]
        self = jnp.logical_and(t == s, home == h)

        @pl.when(jnp.logical_not(self))
        def _():
            remote(block, block, send2.at[0, 0], recv1.at[t], (s, lax.rem(h + 1, m))).wait_recv()

        @pl.when(self)
        def _():
            pltpu.make_async_copy(block, block, local).wait()
        for k in range(1, m):
            remote(block, block, send2.at[t, k - 1], recv2.at[t, k - 1], (s, lax.rem(h + k, m))).start()
        return 0

    lax.fori_loop(0, n, forward, 0)
    lax.fori_loop(2, n // 2, hop, 0)

    def finish(t, _):
        for k in range(1, m):
            block = out_ref.at[t, lax.rem(h + m - k, m)]
            copy = remote(block, block, send2.at[t, k - 1], recv2.at[t, k - 1], (s, lax.rem(h + k, m)))
            copy.wait_recv()
            copy.wait_send()
        return 0

    lax.fori_loop(0, n, finish, 0)

    def drain(i, _):
        p, k = i // m, i % m
        src, owner, g = part(p, k)

        @pl.when(jnp.logical_not(jnp.logical_and(owner == s, k == 0)))
        def _():
            remote(src, out_ref.at[s, g], send1.at[p, k], recv1.at[s], (s, lax.rem(h + 1, m))).wait_send()
        return 0

    lax.fori_loop(0, per * m, drain, 0)
    lax.fori_loop(0, n // 2, settle, 0)
    pltpu.make_async_copy(up_ref, full_ref.at[s], own).wait()


def cost(us):
    return pl.CostEstimate(flops=0, bytes_accessed=int(us * 3.6e6), transcendentals=0)


def params(number):
    return pltpu.CompilerParams(
        collective_id=number, has_side_effects=True, vmem_limit_bytes=32 * 2**20
    )


VMEM = pl.BlockSpec(memory_space=pltpu.VMEM)
ANY = pl.BlockSpec(memory_space=pl.ANY)
DMA = pltpu.SemaphoreType.DMA


def exchange_gated(gated, upstream, n, m):
    per, rows, width = gated.shape
    line = (2, n // 2, PIECES)
    return pl.pallas_call(
        functools.partial(gather_kernel, n, m, per),
        out_shape=(
            jax.ShapeDtypeStruct((n, m, rows // m, width), gated.dtype),
            jax.ShapeDtypeStruct((n,) + upstream.shape, upstream.dtype),
        ),
        in_specs=[VMEM, ANY],
        out_specs=(VMEM, ANY),
        scratch_shapes=[
            DMA((per, m)), DMA((n,)), DMA((n, m - 1)), DMA((n, m - 1)), DMA,
            DMA(line), DMA(line), DMA(line[1:]), DMA(line[1:]), DMA,
        ],
        compiler_params=params(1),
        cost_estimate=cost(45),
    )(gated, upstream)


def scatter_kernel(n, m, per, part_ref, out_ref, land, stage, send1, recv1, send2, recv2, local):
    s, h = lax.axis_index("seq"), lax.axis_index("ch")
    quarter = part_ref.shape[2]
    home, place = s // per, lax.rem(s, per)
    barrier = pltpu.get_barrier_semaphore()
    inside = home == h

    def greet_sender(i, _):
        owner, g = h * per + i // m, i % m

        @pl.when(jnp.logical_not(jnp.logical_and(owner == s, g == h)))
        def _():
            pl.semaphore_signal(barrier, inc=1, device_id=(owner, g), device_id_type=MESH)
        return 0

    lax.fori_loop(0, per * m, greet_sender, 0)
    for k in range(1, m):
        pl.semaphore_signal(barrier, inc=1, device_id=(s, lax.rem(h + k, m)), device_id_type=MESH)
    pl.semaphore_wait(barrier, n + m - 1 - jnp.where(inside, 1, 0))

    def first(i, k):
        t, g = lax.rem(s + i + 1, n), lax.rem(h + k, m)
        return remote(
            part_ref.at[t, g], land.at[i, k - 1], send1.at[i, k - 1], recv1.at[i, k - 1], (s, g)
        )

    def send(i, _):
        for k in range(1, m):
            first(i, k).start()
        return 0

    lax.fori_loop(0, n, send, 0)
    target = out_ref.at[place, pl.ds(pl.multiple_of(h * quarter, quarter), quarter)]

    def combine(i, _):
        t = lax.rem(s + i + 1, n)
        total = part_ref[t, h].astype(jnp.float32)
        for k in range(1, m):
            first(i, k).wait_recv()
        for k in range(1, m):
            total += land[i, k - 1].astype(jnp.float32)
        stage[i] = total.astype(stage.dtype)
        self = jnp.logical_and(t == s, inside)

        @pl.when(jnp.logical_not(self))
        def _():
            remote(stage.at[i], target, send2.at[i], recv2.at[place, h], (t, home)).start()

        @pl.when(self)
        def _():
            pltpu.make_async_copy(stage.at[i], target, local).start()
        return 0

    lax.fori_loop(0, n, combine, 0)

    def finish(i, _):
        t = lax.rem(s + i + 1, n)
        for k in range(1, m):
            first(i, k).wait_send()
        self = jnp.logical_and(t == s, inside)

        @pl.when(jnp.logical_not(self))
        def _():
            remote(stage.at[i], target, send2.at[i], recv2.at[place, h], (s, lax.rem(h + 1, m))).wait_send()

        @pl.when(self)
        def _():
            pltpu.make_async_copy(stage.at[i], target, local).wait()
        return 0

    lax.fori_loop(0, n, finish, 0)

    def arrive(i, _):
        p, g = i // m, i % m
        landed = out_ref.at[p, pl.ds(pl.multiple_of(g * quarter, quarter), quarter)]

        @pl.when(jnp.logical_not(jnp.logical_and(h * per + p == s, g == h)))
        def _():
            remote(landed, landed, send2.at[0], recv2.at[p, g], (s, lax.rem(h + 1, m))).wait_recv()
        return 0

    lax.fori_loop(0, per * m, arrive, 0)


def exchange_grad(part, per):
    n, m, quarter, width = part.shape
    return pl.pallas_call(
        functools.partial(scatter_kernel, n, m, per),
        out_shape=jax.ShapeDtypeStruct((per, m * quarter, width), part.dtype),
        in_specs=[VMEM],
        out_specs=VMEM,
        scratch_shapes=[
            pltpu.VMEM((n, m - 1, quarter, width), part.dtype),
            pltpu.VMEM((n, quarter, width), part.dtype),
            DMA((n, m - 1)), DMA((n, m - 1)), DMA((n,)), DMA((per, m)), DMA,
        ],
        compiler_params=params(2),
        cost_estimate=cost(25),
    )(part)


def sum_kernel(n, local_ref, out_ref, land, send1, recv1, send2, recv2):
    s, h = lax.axis_index("seq"), lax.axis_index("ch")
    barrier = pltpu.get_barrier_semaphore()

    def peer(i):
        return lax.rem(s + i, n)

    def hello(i, _):
        pl.semaphore_signal(barrier, inc=1, device_id=(peer(i), h), device_id_type=MESH)
        return 0

    lax.fori_loop(1, n, hello, 0)
    pl.semaphore_wait(barrier, n - 1)

    def first(i):
        return remote(
            local_ref.at[peer(i)], land.at[i - 1], send1.at[i - 1], recv1.at[i - 1], (peer(i), h)
        )

    def second(i):
        return remote(out_ref.at[s], out_ref.at[s], send2.at[i - 1], recv2.at[i - 1], (peer(i), h))

    def send(i, _):
        first(i).start()
        return 0

    lax.fori_loop(1, n, send, 0)
    total = local_ref[s].astype(jnp.float32)

    def add(i, total):
        first(i).wait_recv()
        return total + land[i - 1].astype(jnp.float32)

    out_ref[s] = lax.fori_loop(1, n, add, total).astype(out_ref.dtype)

    def share(i, _):
        second(i).start()
        return 0

    lax.fori_loop(1, n, share, 0)

    def finish(i, _):
        first(i).wait_send()
        second(i).wait_send()
        landed = out_ref.at[lax.rem(s + n - i, n)]
        remote(landed, landed, send2.at[i - 1], recv2.at[i - 1], (peer(i), h)).wait_recv()
        return 0

    lax.fori_loop(1, n, finish, 0)


def sum_over_seq(value, n):
    blocks = value.astype(jnp.bfloat16).reshape(n, -1, value.shape[1])
    total = pl.pallas_call(
        functools.partial(sum_kernel, n),
        out_shape=jax.ShapeDtypeStruct(blocks.shape, blocks.dtype),
        in_specs=[VMEM],
        out_specs=VMEM,
        scratch_shapes=[
            pltpu.VMEM((n - 1,) + blocks.shape[1:], blocks.dtype),
            DMA((n - 1,)), DMA((n - 1,)), DMA((n - 1,)), DMA((n - 1,)),
        ],
        compiler_params=params(3),
        cost_estimate=cost(15),
    )(blocks)
    return total.reshape(value.shape).astype(value.dtype)


def from_behind(value, axis, steps):
    count = lax.axis_size(axis)
    initial, last = (max(0, -steps), min(count, count - steps))
    return lax.ppermute(value, axis, [(source, source + steps) for source in range(initial, last)])


def depthwise(signal, kernel):
    output = lax.conv_general_dilated(
        signal[None],
        kernel[:, None, :],
        (1,),
        "VALID",
        dimension_numbers=("NWC", "WIO", "NWC"),
        feature_group_count=signal.shape[1],
        precision=lax.Precision.HIGHEST,
    )
    return output[0]


def body(query_stream, key_stream, value_stream, filter_taps, out_weight, upstream):
    rows, channels = query_stream.shape
    tap_count = filter_taps.shape[1]
    n, m, width = lax.axis_size("seq"), lax.axis_size("ch"), out_weight.shape[0]
    per = channels // width
    keyed = (key_stream.astype(jnp.float32) * value_stream.astype(jnp.float32)).astype(jnp.bfloat16)
    rim_before = from_behind(keyed[rows - (tap_count - 1) :], "seq", 1)
    front_pad = jnp.concatenate([rim_before, keyed], axis=0).astype(jnp.float32)
    response = depthwise(front_pad, filter_taps.T[::-1])
    query_wide = query_stream.astype(jnp.float32)
    gated = (query_wide * response).astype(jnp.bfloat16)
    block, upstream_full = exchange_gated(
        gated.reshape(rows, per, width).transpose(1, 0, 2), upstream, n, m
    )
    block = block.reshape(n * rows, width)
    upstream_full = upstream_full.reshape(n * rows, -1)
    mixed_part = jnp.dot(block, out_weight, preferred_element_type=jnp.float32).astype(jnp.bfloat16)

    partial_terms = lax.dot_general(
        upstream_full, out_weight, (((1,), (1,)), ((), ())), preferred_element_type=jnp.float32
    ).astype(jnp.bfloat16)
    partial_terms, mixed_part = lax.optimization_barrier((partial_terms, mixed_part))
    mixed = lax.psum_scatter(mixed_part, "seq", scatter_dimension=0, tiled=True)
    grad_gated = exchange_grad(partial_terms.reshape(n, m, rows // m, width), per)
    grad_gated = grad_gated.transpose(1, 0, 2).reshape(rows, channels).astype(jnp.float32)
    grad_query = (grad_gated * response).astype(jnp.bfloat16)
    grad_response = grad_gated * query_wide
    rim_after = from_behind(grad_response[: tap_count - 1].astype(jnp.bfloat16), "seq", -1)
    rim_after = rim_after.astype(jnp.float32)
    filter_local = depthwise(front_pad, grad_response)[::-1].T
    back_pad = jnp.concatenate([grad_response, rim_after], axis=0)
    grad_keyed = depthwise(back_pad, filter_taps.T)
    filter_local, grad_keyed = lax.optimization_barrier((filter_local, grad_keyed))
    grad_filter = sum_over_seq(filter_local, n)
    grad_key = (grad_keyed * value_stream.astype(jnp.float32)).astype(jnp.bfloat16)
    grad_value = (grad_keyed * key_stream.astype(jnp.float32)).astype(jnp.bfloat16)
    grad_weight = lax.dot_general(
        block, upstream_full, (((0,), (0,)), ((), ())), preferred_element_type=jnp.float32
    )
    return (mixed, grad_query, grad_key, grad_value, grad_filter, grad_weight)


def solution(mesh):
    in_specs = (
        P("seq", "ch"),
        P("seq", "ch"),
        P("seq", "ch"),
        P("ch", None),
        P("seq", "ch"),
        P("seq", "ch"),
    )
    out_specs = (
        P("seq", "ch"),
        P("seq", "ch"),
        P("seq", "ch"),
        P("seq", "ch"),
        P("ch", None),
        P("seq", "ch"),
    )
    return jax.shard_map(body, mesh=mesh, in_specs=in_specs, out_specs=out_specs, check_vma=False)
```

```python
import functools

import jax
import jax.numpy as jnp
from jax import lax
from jax.experimental import pallas as pl
from jax.experimental.pallas import tpu as pltpu
from jax.sharding import PartitionSpec as P

MESH = pl.DeviceIdType.MESH


def remote(src, dst, send, recv, device):
    return pltpu.make_async_remote_copy(
        src_ref=src, dst_ref=dst, send_sem=send, recv_sem=recv, device_id=device, device_id_type=MESH
    )


def greet(devices):
    barrier = pltpu.get_barrier_semaphore()
    for device in devices:
        pl.semaphore_signal(barrier, inc=1, device_id=device, device_id_type=MESH)


PIECES = 2


def gather_kernel(
    n, m, per, gated_ref, up_ref, out_ref, full_ref,
    send1, recv1, send2, recv2, local, send_line, recv_line, send_pair, recv_pair, own,
):
    s, h = lax.axis_index("seq"), lax.axis_index("ch")
    quarter = out_ref.shape[2]
    home = s // per
    barrier = pltpu.get_barrier_semaphore()

    def greet_sender(i, _):
        @pl.when(jnp.logical_not(jnp.logical_and(i == s, home == h)))
        def _():
            pl.semaphore_signal(barrier, inc=1, device_id=(i, home), device_id_type=MESH)
        return 0

    lax.fori_loop(0, n, greet_sender, 0)
    for k in range(1, m):
        pl.semaphore_signal(barrier, inc=1, device_id=(s, lax.rem(h + k, m)), device_id_type=MESH)
    other = s + 1 - 2 * lax.rem(s, 2)
    has_before, has_after = s >= 2, s < n - 2

    pl.semaphore_signal(barrier, inc=1, device_id=(other, h), device_id_type=MESH)

    @pl.when(has_before)
    def _():
        pl.semaphore_signal(barrier, inc=1, device_id=(s - 2, h), device_id_type=MESH)

    @pl.when(has_after)
    def _():
        pl.semaphore_signal(barrier, inc=1, device_id=(s + 2, h), device_id_type=MESH)

    lines = jnp.where(has_before, 1, 0) + jnp.where(has_after, 1, 0)
    pl.semaphore_wait(barrier, per * m + m - jnp.where(home == h, 1, 0) + lines)

    height = up_ref.shape[0] // PIECES

    def shard(t, c):
        return full_ref.at[t, pl.ds(c * height, height)]

    def along(src, t, way, d, c):
        return remote(
            src, shard(t, c), send_line.at[way, d, c], recv_line.at[way, d + 1, c], (s + 2 - 4 * way, h)
        )

    def across(src, t, c):
        return remote(src, shard(t, c), send_pair.at[t // 2, c], recv_pair.at[t // 2, c], (other, h))

    def begin():
        for c in range(PIECES):
            src = up_ref.at[pl.ds(c * height, height)]
            for way, more in enumerate((has_after, has_before)):

                @pl.when(more)
                def _():
                    along(src, s, way, 0, c).start()

            across(src, s, c).start()
        pltpu.make_async_copy(up_ref, full_ref.at[s], own).start()

    def hop(d, _):
        for c in range(PIECES):
            for way, more in enumerate((has_after, has_before)):
                t = s - (2 - 4 * way) * d

                @pl.when(jnp.logical_and(t >= 0, t < n))
                def _():
                    block = shard(t, c)
                    remote(
                        block, block, send_line.at[way, 0, c], recv_line.at[way, d, c], (other, h)
                    ).wait_recv()

                    @pl.when(more)
                    def _():
                        along(block, t, way, d, c).start()

                    across(block, t, c).start()
        return 0

    def settle(d, _):
        for c in range(PIECES):
            for way, more in enumerate((has_after, has_before)):
                t = s - (2 - 4 * way) * d

                @pl.when(jnp.logical_and(jnp.logical_and(t >= 0, t < n), more))
                def _():
                    along(shard(t, c), t, way, d, c).wait_send()

            sent = lax.rem(s, 2) + 2 * d
            across(shard(sent, c), sent, c).wait_send()
            landed = lax.rem(other, 2) + 2 * d
            across(shard(landed, c), landed, c).wait_recv()
        return 0

    def part(p, k):
        g = lax.rem(h + k, m)
        src = gated_ref.at[p, pl.ds(pl.multiple_of(g * quarter, quarter), quarter)]
        return src, h * per + p, g

    def send(i, _):
        p, k = i // m, i % m
        src, owner, g = part(p, k)
        self = jnp.logical_and(owner == s, k == 0)

        @pl.when(jnp.logical_not(self))
        def _():
            remote(src, out_ref.at[s, g], send1.at[p, k], recv1.at[s], (owner, g)).start()

        @pl.when(self)
        def _():
            pltpu.make_async_copy(src, out_ref.at[s, g], local).start()
        return 0

    lax.fori_loop(0, per * m, send, 0)
    begin()
    lax.fori_loop(1, 2, hop, 0)

    def forward(i, _):
        t = lax.rem(s + i, n)
        block = out_ref.at[t, h]
        self = jnp.logical_and(t == s, home == h)

        @pl.when(jnp.logical_not(self))
        def _():
            remote(block, block, send2.at[0, 0], recv1.at[t], (s, lax.rem(h + 1, m))).wait_recv()

        @pl.when(self)
        def _():
            pltpu.make_async_copy(block, block, local).wait()
        for k in range(1, m):
            remote(block, block, send2.at[t, k - 1], recv2.at[t, k - 1], (s, lax.rem(h + k, m))).start()
        return 0

    lax.fori_loop(0, n, forward, 0)
    lax.fori_loop(2, n // 2, hop, 0)

    def finish(t, _):
        for k in range(1, m):
            block = out_ref.at[t, lax.rem(h + m - k, m)]
            copy = remote(block, block, send2.at[t, k - 1], recv2.at[t, k - 1], (s, lax.rem(h + k, m)))
            copy.wait_recv()
            copy.wait_send()
        return 0

    lax.fori_loop(0, n, finish, 0)

    def drain(i, _):
        p, k = i // m, i % m
        src, owner, g = part(p, k)

        @pl.when(jnp.logical_not(jnp.logical_and(owner == s, k == 0)))
        def _():
            remote(src, out_ref.at[s, g], send1.at[p, k], recv1.at[s], (s, lax.rem(h + 1, m))).wait_send()
        return 0

    lax.fori_loop(0, per * m, drain, 0)
    lax.fori_loop(0, n // 2, settle, 0)
    pltpu.make_async_copy(up_ref, full_ref.at[s], own).wait()


def cost(us):
    return pl.CostEstimate(flops=0, bytes_accessed=int(us * 3.6e6), transcendentals=0)


def params(number):
    return pltpu.CompilerParams(
        collective_id=number, has_side_effects=True, vmem_limit_bytes=32 * 2**20
    )


VMEM = pl.BlockSpec(memory_space=pltpu.VMEM)
ANY = pl.BlockSpec(memory_space=pl.ANY)
DMA = pltpu.SemaphoreType.DMA


def exchange_gated(gated, upstream, n, m):
    per, rows, width = gated.shape
    line = (2, n // 2, PIECES)
    return pl.pallas_call(
        functools.partial(gather_kernel, n, m, per),
        out_shape=(
            jax.ShapeDtypeStruct((n, m, rows // m, width), gated.dtype),
            jax.ShapeDtypeStruct((n,) + upstream.shape, upstream.dtype),
        ),
        in_specs=[VMEM, ANY],
        out_specs=(VMEM, ANY),
        scratch_shapes=[
            DMA((per, m)), DMA((n,)), DMA((n, m - 1)), DMA((n, m - 1)), DMA,
            DMA(line), DMA(line), DMA(line[1:]), DMA(line[1:]), DMA,
        ],
        compiler_params=params(1),
        cost_estimate=cost(45),
    )(gated, upstream)


def scatter_kernel(n, m, per, part_ref, out_ref, land, stage, send1, recv1, send2, recv2, local):
    s, h = lax.axis_index("seq"), lax.axis_index("ch")
    quarter = part_ref.shape[2]
    home, place = s // per, lax.rem(s, per)
    barrier = pltpu.get_barrier_semaphore()
    inside = home == h

    def greet_sender(i, _):
        owner, g = h * per + i // m, i % m

        @pl.when(jnp.logical_not(jnp.logical_and(owner == s, g == h)))
        def _():
            pl.semaphore_signal(barrier, inc=1, device_id=(owner, g), device_id_type=MESH)
        return 0

    lax.fori_loop(0, per * m, greet_sender, 0)
    for k in range(1, m):
        pl.semaphore_signal(barrier, inc=1, device_id=(s, lax.rem(h + k, m)), device_id_type=MESH)
    pl.semaphore_wait(barrier, n + m - 1 - jnp.where(inside, 1, 0))

    def first(i, k):
        t, g = lax.rem(s + i + 1, n), lax.rem(h + k, m)
        return remote(
            part_ref.at[t, g], land.at[i, k - 1], send1.at[i, k - 1], recv1.at[i, k - 1], (s, g)
        )

    def send(i, _):
        for k in range(1, m):
            first(i, k).start()
        return 0

    lax.fori_loop(0, n, send, 0)
    target = out_ref.at[place, pl.ds(pl.multiple_of(h * quarter, quarter), quarter)]

    def combine(i, _):
        t = lax.rem(s + i + 1, n)
        total = part_ref[t, h].astype(jnp.float32)
        for k in range(1, m):
            first(i, k).wait_recv()
        for k in range(1, m):
            total += land[i, k - 1].astype(jnp.float32)
        stage[i] = total.astype(stage.dtype)
        self = jnp.logical_and(t == s, inside)

        @pl.when(jnp.logical_not(self))
        def _():
            remote(stage.at[i], target, send2.at[i], recv2.at[place, h], (t, home)).start()

        @pl.when(self)
        def _():
            pltpu.make_async_copy(stage.at[i], target, local).start()
        return 0

    lax.fori_loop(0, n, combine, 0)

    def finish(i, _):
        t = lax.rem(s + i + 1, n)
        for k in range(1, m):
            first(i, k).wait_send()
        self = jnp.logical_and(t == s, inside)

        @pl.when(jnp.logical_not(self))
        def _():
            remote(stage.at[i], target, send2.at[i], recv2.at[place, h], (s, lax.rem(h + 1, m))).wait_send()

        @pl.when(self)
        def _():
            pltpu.make_async_copy(stage.at[i], target, local).wait()
        return 0

    lax.fori_loop(0, n, finish, 0)

    def arrive(i, _):
        p, g = i // m, i % m
        landed = out_ref.at[p, pl.ds(pl.multiple_of(g * quarter, quarter), quarter)]

        @pl.when(jnp.logical_not(jnp.logical_and(h * per + p == s, g == h)))
        def _():
            remote(landed, landed, send2.at[0], recv2.at[p, g], (s, lax.rem(h + 1, m))).wait_recv()
        return 0

    lax.fori_loop(0, per * m, arrive, 0)


def exchange_grad(part, per):
    n, m, quarter, width = part.shape
    return pl.pallas_call(
        functools.partial(scatter_kernel, n, m, per),
        out_shape=jax.ShapeDtypeStruct((per, m * quarter, width), part.dtype),
        in_specs=[VMEM],
        out_specs=VMEM,
        scratch_shapes=[
            pltpu.VMEM((n, m - 1, quarter, width), part.dtype),
            pltpu.VMEM((n, quarter, width), part.dtype),
            DMA((n, m - 1)), DMA((n, m - 1)), DMA((n,)), DMA((per, m)), DMA,
        ],
        compiler_params=params(2),
        cost_estimate=cost(25),
    )(part)


def sum_kernel(n, local_ref, out_ref, land, send1, recv1, send2, recv2):
    s, h = lax.axis_index("seq"), lax.axis_index("ch")
    barrier = pltpu.get_barrier_semaphore()

    def peer(i):
        return lax.rem(s + i, n)

    def hello(i, _):
        pl.semaphore_signal(barrier, inc=1, device_id=(peer(i), h), device_id_type=MESH)
        return 0

    lax.fori_loop(1, n, hello, 0)
    pl.semaphore_wait(barrier, n - 1)

    def first(i):
        return remote(
            local_ref.at[peer(i)], land.at[i - 1], send1.at[i - 1], recv1.at[i - 1], (peer(i), h)
        )

    def second(i):
        return remote(out_ref.at[s], out_ref.at[s], send2.at[i - 1], recv2.at[i - 1], (peer(i), h))

    def send(i, _):
        first(i).start()
        return 0

    lax.fori_loop(1, n, send, 0)
    total = local_ref[s].astype(jnp.float32)

    def add(i, total):
        first(i).wait_recv()
        return total + land[i - 1].astype(jnp.float32)

    out_ref[s] = lax.fori_loop(1, n, add, total).astype(out_ref.dtype)

    def share(i, _):
        second(i).start()
        return 0

    lax.fori_loop(1, n, share, 0)

    def finish(i, _):
        first(i).wait_send()
        second(i).wait_send()
        landed = out_ref.at[lax.rem(s + n - i, n)]
        remote(landed, landed, send2.at[i - 1], recv2.at[i - 1], (peer(i), h)).wait_recv()
        return 0

    lax.fori_loop(1, n, finish, 0)


def sum_over_seq(value, n):
    blocks = value.astype(jnp.bfloat16).reshape(n, -1, value.shape[1])
    total = pl.pallas_call(
        functools.partial(sum_kernel, n),
        out_shape=jax.ShapeDtypeStruct(blocks.shape, blocks.dtype),
        in_specs=[VMEM],
        out_specs=VMEM,
        scratch_shapes=[
            pltpu.VMEM((n - 1,) + blocks.shape[1:], blocks.dtype),
            DMA((n - 1,)), DMA((n - 1,)), DMA((n - 1,)), DMA((n - 1,)),
        ],
        compiler_params=params(3),
        cost_estimate=cost(15),
    )(blocks)
    return total.reshape(value.shape).astype(value.dtype)


def from_behind(value, axis, steps):
    count = lax.axis_size(axis)
    initial, last = (max(0, -steps), min(count, count - steps))
    return lax.ppermute(value, axis, [(source, source + steps) for source in range(initial, last)])


def depthwise(signal, kernel):
    output = lax.conv_general_dilated(
        signal[None],
        kernel[:, None, :],
        (1,),
        "VALID",
        dimension_numbers=("NWC", "WIO", "NWC"),
        feature_group_count=signal.shape[1],
        precision=lax.Precision.HIGHEST,
    )
    return output[0]


def body(query_stream, key_stream, value_stream, filter_taps, out_weight, upstream):
    rows, channels = query_stream.shape
    tap_count = filter_taps.shape[1]
    n, m, width = lax.axis_size("seq"), lax.axis_size("ch"), out_weight.shape[0]
    per = channels // width
    keyed = (key_stream.astype(jnp.float32) * value_stream.astype(jnp.float32)).astype(jnp.bfloat16)
    rim_before = from_behind(keyed[rows - (tap_count - 1) :], "seq", 1)
    front_pad = jnp.concatenate([rim_before, keyed], axis=0).astype(jnp.float32)
    response = depthwise(front_pad, filter_taps.T[::-1])
    query_wide = query_stream.astype(jnp.float32)
    gated = (query_wide * response).astype(jnp.bfloat16)
    block, upstream_full = exchange_gated(
        gated.reshape(rows, per, width).transpose(1, 0, 2), upstream, n, m
    )
    block = block.reshape(n * rows, width)
    upstream_full = upstream_full.reshape(n * rows, -1)
    mixed_part = jnp.dot(block, out_weight, preferred_element_type=jnp.float32).astype(jnp.bfloat16)
    mixed_part, upstream_full = lax.optimization_barrier((mixed_part, upstream_full))

    partial_terms = lax.dot_general(
        upstream_full, out_weight, (((1,), (1,)), ((), ())), preferred_element_type=jnp.float32
    ).astype(jnp.bfloat16)
    mixed = lax.psum_scatter(mixed_part, "seq", scatter_dimension=0, tiled=True)
    grad_gated = exchange_grad(partial_terms.reshape(n, m, rows // m, width), per)
    grad_gated = grad_gated.transpose(1, 0, 2).reshape(rows, channels).astype(jnp.float32)
    grad_query = (grad_gated * response).astype(jnp.bfloat16)
    grad_response = grad_gated * query_wide
    rim_after = from_behind(grad_response[: tap_count - 1].astype(jnp.bfloat16), "seq", -1)
    rim_after = rim_after.astype(jnp.float32)
    filter_local = depthwise(front_pad, grad_response)[::-1].T
    back_pad = jnp.concatenate([grad_response, rim_after], axis=0)
    grad_keyed = depthwise(back_pad, filter_taps.T)
    filter_local, grad_keyed = lax.optimization_barrier((filter_local, grad_keyed))
    grad_filter = sum_over_seq(filter_local, n)
    grad_key = (grad_keyed * value_stream.astype(jnp.float32)).astype(jnp.bfloat16)
    grad_value = (grad_keyed * key_stream.astype(jnp.float32)).astype(jnp.bfloat16)
    grad_weight = lax.dot_general(
        block, upstream_full, (((0,), (0,)), ((), ())), preferred_element_type=jnp.float32
    )
    return (mixed, grad_query, grad_key, grad_value, grad_filter, grad_weight)


def solution(mesh):
    in_specs = (
        P("seq", "ch"),
        P("seq", "ch"),
        P("seq", "ch"),
        P("ch", None),
        P("seq", "ch"),
        P("seq", "ch"),
    )
    out_specs = (
        P("seq", "ch"),
        P("seq", "ch"),
        P("seq", "ch"),
        P("seq", "ch"),
        P("ch", None),
        P("seq", "ch"),
    )
    return jax.shard_map(body, mesh=mesh, in_specs=in_specs, out_specs=out_specs, check_vma=False)
```
